32 devices in a mesh: mp: 2 (over core), feat: 16 (over z, y, x).
Axes of the slice: x: 2, y: 2, z: 4, core: 2. Of those that a mesh axis runs over, the one named last changes fastest.
Arguments:
- target_ids: int32 [16], replicated, may hold values from 0 to 127999
- target_pos: int32 [16], replicated, may hold values from 24 to 47
- unembed: bfloat16 [128000, 2304], P(('mp', 'feat')), may hold values from -6 to 6
- attn_weights: float32 [8, 16, 48, 48], P('mp'), may hold values from 0.02 to 1
- inv_rms: float32 [16, 48], replicated, may hold values from 0.5 to 2
- norm_gain: float32 [2304], replicated, may hold values from 0.1 to 1.9
- w_value: bfloat16 [4, 2304, 256], P(None, 'mp'), may hold values from -0.125 to 0.125
- w_out: bfloat16 [8, 256, 2304], P('mp'), may hold values from -0.375 to 0.375
- decoder: bfloat16 [2, 98304, 2304], P(None, ('mp', 'feat')), may hold values from -0.125 to 0.125
- activation: bfloat16 [16, 48, 98304], P(None, None, ('mp', 'feat')), may hold values from 0.5 to 4
- active: int32 [16, 48, 98304], P(None, None, ('mp', 'feat')), may hold values 0 or 1
Outputs:
- attribution: float32 [16, 48, 98304], P(None, None, ('mp', 'feat'))
The draws below stay inside these ranges and needn't reach their ends.
All inputs are finite; a program needn't handle non-finite values. No bound on the sum of `active` on one device may be relied on, other than what follows from the above.
Results may differ from the reference program's by a relative error of at most 0.0035.
Values may be sent and summed in bfloat16 or wider, within the bound.
A program may use at most 128 MiB of HBM per device.

```python
import math
import jax
import jax.numpy as jnp
from jax import lax

D = 2304
HEADS = 8
KV = 4
HD = 256
FEATS = 98304
VOCAB = 128000
REACH = 2
TARGETS = 16
POS = 48


def set_ends(values, rng, least, largest):
    index_at = [jax.random.randint(jax.random.fold_in(rng, axis), (), 0, length) for axis, length in enumerate(values.shape)]
    widest = values.shape.index(max(values.shape))
    beside = index_at[:widest] + [(index_at[widest] + 1) % values.shape[widest]] + index_at[widest + 1:]
    return values.at[tuple(index_at)].set(least).at[tuple(beside)].set(largest)


def block_scale(key, extent, shards, least, largest):
    loudness, own = 1.0, jax.random.fold_in(key, 6)
    for dim, parts in shards:
        steps = jnp.exp(jax.random.uniform(jax.random.fold_in(own, dim), (parts,), jnp.float32, least / len(shards), largest / len(shards)))
        loudness = loudness * jnp.repeat(steps, extent[dim] // parts).reshape([-1 if axis == dim else 1 for axis in range(len(extent))])
    return loudness


def normal_values(key, shape, deviation, limit, shards=(), kind=jnp.bfloat16):
    entries = deviation * jax.random.normal(key, shape, jnp.float32)
    if shards:
        entries = entries * block_scale(key, shape, shards, -0.22, 0.18)
    return jnp.clip(entries, -limit, limit).astype(kind)


def setup_inputs(seed: int = 0) -> dict:
    seeds = jax.random.split(jax.random.key(seed), 12)
    target_ids = set_ends(jax.random.randint(seeds[0], (TARGETS,), 0, VOCAB), jax.random.fold_in(seeds[0], 1), 0, VOCAB - 1).astype(jnp.int32)
    target_pos = set_ends(jax.random.randint(seeds[1], (TARGETS,), POS // 2, POS), jax.random.fold_in(seeds[1], 1), POS // 2, POS - 1).astype(jnp.int32)
    unembed = normal_values(seeds[2], (VOCAB, D), 1.0, 6.0, ((0, 32),))
    attn_weights = jnp.clip(jnp.exp(math.log(1.0) - 3.912023 * jax.random.uniform(seeds[3], (HEADS, TARGETS, POS, POS), jnp.float32) ** block_scale(seeds[3], (HEADS, TARGETS, POS, POS), ((0, 2),), -0.2, 0.2)), 0.02, 1.0)
    inv_rms = jnp.clip(jnp.exp(jax.random.uniform(seeds[4], (TARGETS, POS), jnp.float32, math.log(0.5), math.log(2.0))), 0.5, 2.0)
    norm_gain = jnp.clip(1.0 + 0.18 * jax.random.normal(seeds[5], (D,), jnp.float32), 0.1, 1.9)
    w_value = normal_values(seeds[6], (KV, D, HD), D ** -0.5, 0.125, ((1, 2),))
    w_out = normal_values(seeds[7], (HEADS, HD, D), HD ** -0.5, 0.375, ((0, 2),))
    decoder = normal_values(seeds[8], (REACH, FEATS, D), D ** -0.5, 0.125, ((1, 32),))
    activation = jnp.clip(jnp.exp(math.log(4.0) - 2.0794415 * jax.random.uniform(seeds[9], (TARGETS, POS, FEATS), jnp.float32) ** block_scale(seeds[9], (TARGETS, POS, FEATS), ((2, 32),), -0.2, 0.2)), 0.5, 4.0).astype(jnp.bfloat16)
    active = set_ends((jax.random.randint(seeds[10], (TARGETS, POS, FEATS), 0, 4) < 1).astype(jnp.int32), jax.random.fold_in(seeds[10], 1), 0, 1)
    return {"target_ids": target_ids, "target_pos": target_pos, "unembed": unembed, "attn_weights": attn_weights, "inv_rms": inv_rms, "norm_gain": norm_gain, "w_value": w_value, "w_out": w_out, "decoder": decoder, "activation": activation, "active": active}


def reference(target_ids, target_pos, unembed, attn_weights, inv_rms, norm_gain, w_value, w_out, decoder, activation, active):
    row_count = TARGETS * POS
    direction = jnp.take(unembed, target_ids, axis=0).astype(jnp.float32)
    placing = (jnp.arange(POS, dtype=jnp.int32)[None, :] == target_pos[:, None]).astype(jnp.float32)
    upper = (placing[:, :, None] * direction[:, None, :]).reshape(row_count, D)
    lowered_top = upper.astype(jnp.bfloat16)
    index_pos = jnp.arange(POS, dtype=jnp.int32)
    causal = (index_pos[:, None] >= index_pos[None, :]).astype(jnp.float32)
    weights = attn_weights * causal
    pattern = weights / jnp.sum(weights, axis=-1, keepdims=True)
    group_size = HEADS // KV
    lowered_wide = lowered_top.astype(jnp.float32).reshape(TARGETS, POS, D)
    heads_sum = jnp.zeros((row_count, D), jnp.float32)
    for head_index in range(HEADS):
        mixed = jnp.einsum("gts,gtd->gsd", pattern[head_index], lowered_wide, precision=lax.Precision.HIGHEST)
        mixed = mixed.reshape(row_count, D).astype(jnp.bfloat16)
        spread = jnp.dot(mixed, w_out[head_index].T, preferred_element_type=jnp.float32).astype(jnp.bfloat16)
        heads_sum = heads_sum + jnp.dot(spread, w_value[head_index // group_size].T, preferred_element_type=jnp.float32)
    below = upper + inv_rms.reshape(row_count, 1) * norm_gain[None, :] * heads_sum
    lowered_bottom = below.astype(jnp.bfloat16)
    scores = jnp.dot(lowered_bottom, decoder[0].T, preferred_element_type=jnp.float32)
    scores = scores + jnp.dot(lowered_top, decoder[1].T, preferred_element_type=jnp.float32)
    attribution = activation.astype(jnp.float32).reshape(row_count, FEATS) * active.reshape(row_count, FEATS).astype(jnp.float32) * scores
    return attribution.reshape(TARGETS, POS, FEATS)
```

```python
import functools

import jax
import jax.numpy as jnp
from jax import lax
from jax.experimental import pallas as pl
from jax.experimental.pallas import tpu as pltpu
from jax.sharding import PartitionSpec as P

MESH = pl.DeviceIdType.MESH
NT = (((1,), (1,)), ((), ()))
TILE = 16


def bits_of(n):
    return [1 << b for b in range(n.bit_length() - 1)]


def flip(index, bit):
    return index + bit - 2 * bit * lax.rem(lax.div(index, bit), 2)


def chunk_of(n, most):
    return max(c for c in range(TILE, most + 1, TILE) if n % c == 0)


def pick_kernel(ids, unembed, dir_ref, blocks, sems):
    rows, width = unembed.shape
    targets = dir_ref.shape[1]
    half = width // 2
    rank = lax.axis_index("mp") * lax.axis_size("feat") + lax.axis_index("feat")
    first = rank * rows

    def fetch(g):
        local = jnp.clip(ids[g] - first, 0, rows - 1)
        base = pl.multiple_of(lax.div(local, TILE) * TILE, TILE)
        return pltpu.make_async_copy(
            unembed.at[pl.ds(base, TILE), :],
            blocks.at[pl.ds(g * TILE, TILE), :],
            sems.at[g],
        )

    for g in range(targets):
        fetch(g).start()
    lane = lax.broadcasted_iota(jnp.int32, (targets, targets * TILE), 1)
    row = lax.broadcasted_iota(jnp.int32, (targets, targets * TILE), 0)
    picker = jnp.zeros((targets, targets * TILE), jnp.float32)
    for g in range(targets):
        local = ids[g] - first
        inside = (local >= 0) & (local < rows)
        at = jnp.where(inside, g * TILE + lax.rem(jnp.maximum(local, 0), TILE), -1)
        picker = jnp.where((row == g) & (lane == at), 1.0, picker)
    for g in range(targets):
        fetch(g).wait()
    picker = picker.astype(jnp.bfloat16)
    for c in range(2):
        dir_ref[c] = jnp.dot(
            picker, blocks[:, pl.ds(c * half, half)], preferred_element_type=jnp.float32
        ).astype(jnp.bfloat16)


def place_coefficients(pos, attn, inv_rms, ct_ref):
    heads, targets, positions, _ = attn.shape
    total = targets * positions
    spots = lax.broadcasted_iota(jnp.int32, (positions, total), 1) - lax.broadcasted_iota(
        jnp.int32, (positions, total), 0
    )
    tile = jnp.zeros((positions, total), jnp.float32)
    for g in range(targets):
        tile = jnp.where(spots == g * positions, 1.0, tile)
    lane = lax.broadcasted_iota(jnp.int32, (targets, total), 1)
    row = lax.broadcasted_iota(jnp.int32, (targets, total), 0)
    own = (lane >= row * positions) & (lane < (row + 1) * positions)
    t_iota = lax.broadcasted_iota(jnp.int32, (positions, positions), 0)
    s_row = lax.broadcasted_iota(jnp.int32, (1, positions), 1)
    for h in range(heads):
        lines = []
        for g in range(targets):
            line = jnp.sum(
                jnp.where(t_iota == pos[g], attn[h, g], 0.0), axis=0, keepdims=True
            )
            lines.append(jnp.where(s_row <= pos[g], line, 0.0))
        weights = jnp.concatenate(lines, axis=0)
        pattern = weights / jnp.sum(weights, axis=-1, keepdims=True) * inv_rms[...]
        spreadout = jnp.dot(
            pattern, tile, precision=lax.Precision.HIGHEST, preferred_element_type=jnp.float32
        )
        ct_ref[pl.ds(h * targets, targets), :] = jnp.where(own, spreadout, 0.0).astype(
            jnp.bfloat16
        )


def target_rows(pos, targets, positions):
    total = targets * positions
    lane = lax.broadcasted_iota(jnp.int32, (targets, total), 1)
    row = lax.broadcasted_iota(jnp.int32, (targets, total), 0)
    delta = jnp.zeros((targets, total), jnp.float32)
    for g in range(targets):
        delta = jnp.where((row == g) & (lane == g * positions + pos[g]), 1.0, delta)
    return delta


def share_kernel(
    n_mp,
    n_feat,
    pos,
    dir_ref,
    attn,
    inv_rms,
    gain_ref,
    w_out,
    w_value,
    lower,
    c_ref,
    pair_in,
    acc,
    got,
    dir_full,
    attn_v,
    w_out_v,
    w_full,
    u_all,
    ct_own,
    ct_all,
    pair_sem,
    step_send,
    step_recv,
    full_sem,
    w_sem,
    gather_send,
    gather_recv,
):
    mp = lax.axis_index("mp")
    feat = lax.axis_index("feat")
    mine = lax.rem(mp, 2)
    other = 1 - mine
    pair = {"mp": flip(mp, 1)}
    stages = [("feat", b) for b in bits_of(n_feat)] + [("mp", b) for b in bits_of(n_mp)[1:]]
    count, pieces = len(stages), got.shape[1]
    targets = dir_ref.shape[1]
    half = dir_ref.shape[2]
    width = 2 * half
    local_heads = w_out.shape[0]
    kv_heads, columns, head_size = w_value.shape
    heads = local_heads * n_mp

    own_columns = pl.ds(pl.multiple_of(mp * columns, TILE), columns)
    load_attn = pltpu.make_async_copy(attn, attn_v, w_sem.at[2])
    load_out = pltpu.make_async_copy(w_out, w_out_v, w_sem.at[0])
    load_value = pltpu.make_async_copy(w_value, w_full.at[:, own_columns, :], w_sem.at[1])
    load_attn.start()
    load_out.start()
    load_value.start()

    def partner(stage):
        axis, bit = stages[stage]
        return {axis: flip(feat if axis == "feat" else mp, bit)}

    barrier = pltpu.get_barrier_semaphore()
    greeted = [{"feat": flip(feat, b)} for b in bits_of(n_feat)]
    greeted += [{"mp": lax.rem(mp + o, n_mp)} for o in range(1, n_mp)]
    for device in greeted:
        pl.semaphore_signal(barrier, inc=1, device_id=device, device_id_type=MESH)
    pl.semaphore_wait(barrier, len(greeted))

    def remote(src, dst, send, recv, device):
        copy = pltpu.make_async_remote_copy(
            src_ref=src,
            dst_ref=dst,
            send_sem=send,
            recv_sem=recv,
            device_id=device,
            device_id_type=MESH,
        )
        copy.start()
        return copy

    def gather(kind, src, dst):
        return [
            remote(
                src,
                dst,
                gather_send.at[kind, o - 1],
                gather_recv.at[kind, o - 1],
                {"mp": lax.rem(mp + o, n_mp)},
            )
            for o in range(1, n_mp)
        ]

    first = remote(dir_ref.at[other], pair_in, pair_sem.at[0], pair_sem.at[1], pair)
    values_sent = gather(0, w_value, w_full.at[:, own_columns, :])
    first.wait()
    start = dir_ref[mine] + pair_in[...]
    size = half // pieces
    for p in range(pieces):
        acc[0, p] = start[:, p * size : (p + 1) * size]
    coefficients_sent = []
    for k in range(count):
        copies = []
        for p in range(pieces):
            copies.append(
                remote(
                    acc.at[k, p],
                    got.at[k, p],
                    step_send.at[k, p],
                    step_recv.at[k, p],
                    partner((k + p) % count),
                )
            )
        if k == 0:
            load_attn.wait()
            place_coefficients(pos, attn_v, inv_rms, ct_own)
            coefficients_sent = gather(1, ct_own, ct_all.at[mp])
            ct_all[mp] = ct_own[...]
        for p in range(pieces):
            copies[p].wait()
            acc[k + 1, p] = acc[k, p] + got[k, p]
    for p in range(pieces):
        dir_full[mine, :, p * size : (p + 1) * size] = acc[count, p]
    last = remote(
        dir_full.at[mine], dir_full.at[mine], full_sem.at[0], full_sem.at[1], pair
    )
    load_out.wait()
    last.wait()

    for c in range(2):
        part = dir_full[c]
        lower[pl.ds(heads * targets, targets), pl.ds(c * half, half)] = part
        lower[pl.ds((heads + 1) * targets, targets), pl.ds(c * half, half)] = part
    direction = lower[pl.ds(heads * targets, targets), :]
    own_u = lax.dot_general(
        direction,
        w_out_v[...].reshape(local_heads * head_size, width),
        NT,
        preferred_element_type=jnp.float32,
    ).astype(jnp.bfloat16)
    for l in range(local_heads):
        u_all[mp, l] = own_u[:, l * head_size : (l + 1) * head_size]
    u_sent = gather(2, u_all.at[mp], u_all.at[mp])

    for copy in coefficients_sent:
        copy.wait()
    delta = target_rows(pos, targets, inv_rms.shape[1])
    coefficients = jnp.concatenate(
        [ct_all[m].astype(jnp.float32) for m in range(n_mp)] + [delta] * 2, axis=0
    )
    c_ref[...] = coefficients.T.astype(jnp.bfloat16)
    load_value.wait()
    for copy in values_sent:
        copy.wait()
    for copy in u_sent:
        copy.wait()
    group = heads // kv_heads
    gain = gain_ref[...].reshape(1, width)
    for kv in range(kv_heads):
        spread = jnp.concatenate(
            [
                u_all[h // local_heads, h % local_heads]
                for h in range(kv * group, (kv + 1) * group)
            ],
            axis=0,
        )
        value = lax.dot_general(spread, w_full[kv], NT, preferred_element_type=jnp.float32)
        lower[pl.ds(kv * group * targets, group * targets), :] = (value * gain).astype(
            jnp.bfloat16
        )


def gate_kernel(straight, c_ref, lower, dec, act_ref, on_ref, out_ref):
    rank_rows = lower.shape[0]
    top_row = rank_rows - straight
    bottom = lax.dot_general(dec[0], lower[...], NT, preferred_element_type=jnp.float32)
    top = lax.dot_general(
        dec[1], lower[pl.ds(top_row, straight), :], NT, preferred_element_type=jnp.float32
    )
    both = bottom[:, top_row:] + top
    high = both.astype(jnp.bfloat16).astype(jnp.float32)
    lane = lax.broadcasted_iota(jnp.int32, both.shape, 1)
    low = jnp.where(lane < straight // 2, high, both - high)
    z = jnp.concatenate([bottom[:, :top_row], low], axis=1).astype(jnp.bfloat16)
    scores = lax.dot_general(c_ref[...], z, NT, preferred_element_type=jnp.float32)
    out_ref[...] = act_ref[...].astype(jnp.float32) * on_ref[...].astype(jnp.float32) * scores


def on_device(
    n_mp,
    n_feat,
    target_ids,
    target_pos,
    unembed,
    attn_weights,
    inv_rms,
    norm_gain,
    w_value,
    w_out,
    decoder,
    activation,
    active,
):
    vocab_rows, width = unembed.shape
    targets, positions = inv_rms.shape
    local_heads = w_out.shape[0]
    kv_heads, columns, head_size = w_value.shape
    features = decoder.shape[1]
    total = targets * positions
    half = width // 2
    heads = local_heads * n_mp
    rank_rows = heads * targets + 2 * targets
    bf16, f32 = jnp.bfloat16, jnp.float32
    vmem = pl.BlockSpec(memory_space=pltpu.VMEM)
    smem = pl.BlockSpec(memory_space=pltpu.SMEM)
    hbm = pl.BlockSpec(memory_space=pl.ANY)

    if vocab_rows % TILE:
        unembed = jnp.pad(unembed, ((0, TILE - vocab_rows % TILE), (0, 0)))
        rank = lax.axis_index("mp") * n_feat + lax.axis_index("feat")
        local = target_ids - rank * vocab_rows
        inside = (local >= 0) & (local < vocab_rows)
        target_ids = jnp.where(inside, rank * unembed.shape[0] + local, -1)
    direction = pl.pallas_call(
        pick_kernel,
        out_shape=jax.ShapeDtypeStruct((2, targets, half), bf16),
        in_specs=[smem, hbm],
        out_specs=vmem,
        scratch_shapes=[
            pltpu.VMEM((targets * TILE, width), bf16),
            pltpu.SemaphoreType.DMA((targets,)),
        ],
        compiler_params=pltpu.CompilerParams(vmem_limit_bytes=63 * 2**20),
        cost_estimate=pl.CostEstimate(
            flops=2 * targets * targets * TILE * width,
            bytes_accessed=2 * targets * TILE * width,
            transcendentals=0,
        ),
        name="pick_rows",
    )(target_ids, unembed)

    steps = len(bits_of(n_feat)) + len(bits_of(n_mp)) - 1
    pieces = 3 if half % (3 * 128) == 0 else 1
    size = half // pieces
    dma = pltpu.SemaphoreType.DMA
    lower, c = pl.pallas_call(
        functools.partial(share_kernel, n_mp, n_feat),
        out_shape=(
            jax.ShapeDtypeStruct((rank_rows, width), bf16),
            jax.ShapeDtypeStruct((total, rank_rows), bf16),
        ),
        in_specs=[smem, vmem, hbm, vmem, vmem, hbm, hbm],
        out_specs=(vmem, vmem),
        scratch_shapes=[
            pltpu.VMEM((targets, half), bf16),
            pltpu.VMEM((steps + 1, pieces, targets, size), bf16),
            pltpu.VMEM((steps, pieces, targets, size), bf16),
            pltpu.VMEM((2, targets, half), bf16),
            pltpu.VMEM(attn_weights.shape, f32),
            pltpu.VMEM(w_out.shape, bf16),
            pltpu.VMEM((kv_heads, columns * n_mp, head_size), bf16),
            pltpu.VMEM((n_mp, local_heads, targets, head_size), bf16),
            pltpu.VMEM((local_heads * targets, total), bf16),
            pltpu.VMEM((n_mp, local_heads * targets, total), bf16),
            dma((2,)),
            dma((steps, pieces)),
            dma((steps, pieces)),
            dma((2,)),
            dma((3,)),
            dma((3, n_mp - 1)),
            dma((3, n_mp - 1)),
        ],
        compiler_params=pltpu.CompilerParams(
            collective_id=0, has_side_effects=True, vmem_limit_bytes=63 * 2**20
        ),
        cost_estimate=pl.CostEstimate(
            flops=2 * features * width * rank_rows,
            bytes_accessed=4 * features * width + 6 * total * features,
            transcendentals=0,
        ),
        name="share",
    )(target_pos, direction, attn_weights, inv_rms, norm_gain, w_out, w_value)

    chunk = chunk_of(features, 384)
    out = pl.pallas_call(
        functools.partial(gate_kernel, 2 * targets),
        grid=(features // chunk,),
        out_shape=jax.ShapeDtypeStruct((total, features), f32),
        in_specs=[
            pl.BlockSpec((total, rank_rows), lambda i: (0, 0)),
            pl.BlockSpec((rank_rows, width), lambda i: (0, 0)),
            pl.BlockSpec((2, chunk, width), lambda i: (0, i, 0)),
            pl.BlockSpec((total, chunk), lambda i: (0, i)),
            pl.BlockSpec((total, chunk), lambda i: (0, i)),
        ],
        out_specs=pl.BlockSpec((total, chunk), lambda i: (0, i)),
        compiler_params=pltpu.CompilerParams(vmem_limit_bytes=63 * 2**20),
        cost_estimate=pl.CostEstimate(
            flops=2 * features * (width + total) * rank_rows,
            bytes_accessed=10 * total * features + 4 * features * width,
            transcendentals=0,
        ),
        name="score_and_gate",
    )(c, lower, decoder, activation.reshape(total, features), active.reshape(total, features))
    return out.reshape(targets, positions, features)


def solution(mesh):
    in_specs = (
        P(),
        P(),
        P(("mp", "feat"), None),
        P("mp", None, None, None),
        P(),
        P(),
        P(None, "mp", None),
        P("mp", None, None),
        P(None, ("mp", "feat"), None),
        P(None, None, ("mp", "feat")),
        P(None, None, ("mp", "feat")),
    )
    out_specs = P(None, None, ("mp", "feat"))
    return jax.shard_map(
        functools.partial(on_device, mesh.shape["mp"], mesh.shape["feat"]),
        mesh=mesh,
        in_specs=in_specs,
        out_specs=out_specs,
        check_vma=False,
    )
```

```python
import functools

import jax
import jax.numpy as jnp
from jax import lax
from jax.experimental import pallas as pl
from jax.experimental.pallas import tpu as pltpu
from jax.sharding import PartitionSpec as P

MESH = pl.DeviceIdType.MESH
NT = (((1,), (1,)), ((), ()))
TILE = 16


def bits_of(n):
    return [1 << b for b in range(n.bit_length() - 1)]


def flip(index, bit):
    return index + bit - 2 * bit * lax.rem(lax.div(index, bit), 2)


def chunk_of(n, most):
    return max(c for c in range(TILE, most + 1, TILE) if n % c == 0)


def pick_kernel(ids, unembed, dir_ref, blocks, sems):
    rows, width = unembed.shape
    targets = dir_ref.shape[1]
    half = width // 2
    rank = lax.axis_index("mp") * lax.axis_size("feat") + lax.axis_index("feat")
    first = rank * rows

    def fetch(g):
        local = jnp.clip(ids[g] - first, 0, rows - 1)
        base = pl.multiple_of(lax.div(local, TILE) * TILE, TILE)
        return pltpu.make_async_copy(
            unembed.at[pl.ds(base, TILE), :],
            blocks.at[pl.ds(g * TILE, TILE), :],
            sems.at[g],
        )

    for g in range(targets):
        fetch(g).start()
    lane = lax.broadcasted_iota(jnp.int32, (targets, targets * TILE), 1)
    row = lax.broadcasted_iota(jnp.int32, (targets, targets * TILE), 0)
    picker = jnp.zeros((targets, targets * TILE), jnp.float32)
    for g in range(targets):
        local = ids[g] - first
        inside = (local >= 0) & (local < rows)
        at = jnp.where(inside, g * TILE + lax.rem(jnp.maximum(local, 0), TILE), -1)
        picker = jnp.where((row == g) & (lane == at), 1.0, picker)
    for g in range(targets):
        fetch(g).wait()
    picker = picker.astype(jnp.bfloat16)
    for c in range(2):
        dir_ref[c] = jnp.dot(
            picker, blocks[:, pl.ds(c * half, half)], preferred_element_type=jnp.float32
        ).astype(jnp.bfloat16)


def place_coefficients(pos, attn, inv_rms, ct_ref):
    heads, targets, positions, _ = attn.shape
    total = targets * positions
    spots = lax.broadcasted_iota(jnp.int32, (positions, total), 1) - lax.broadcasted_iota(
        jnp.int32, (positions, total), 0
    )
    tile = jnp.zeros((positions, total), jnp.float32)
    for g in range(targets):
        tile = jnp.where(spots == g * positions, 1.0, tile)
    lane = lax.broadcasted_iota(jnp.int32, (targets, total), 1)
    row = lax.broadcasted_iota(jnp.int32, (targets, total), 0)
    own = (lane >= row * positions) & (lane < (row + 1) * positions)
    t_iota = lax.broadcasted_iota(jnp.int32, (positions, positions), 0)
    s_row = lax.broadcasted_iota(jnp.int32, (1, positions), 1)
    for h in range(heads):
        lines = []
        for g in range(targets):
            line = jnp.sum(
                jnp.where(t_iota == pos[g], attn[h, g], 0.0), axis=0, keepdims=True
            )
            lines.append(jnp.where(s_row <= pos[g], line, 0.0))
        weights = jnp.concatenate(lines, axis=0)
        pattern = weights / jnp.sum(weights, axis=-1, keepdims=True) * inv_rms[...]
        spreadout = jnp.dot(
            pattern, tile, precision=lax.Precision.HIGHEST, preferred_element_type=jnp.float32
        )
        ct_ref[pl.ds(h * targets, targets), :] = jnp.where(own, spreadout, 0.0).astype(
            jnp.bfloat16
        )


def target_rows(pos, targets, positions):
    total = targets * positions
    lane = lax.broadcasted_iota(jnp.int32, (targets, total), 1)
    row = lax.broadcasted_iota(jnp.int32, (targets, total), 0)
    delta = jnp.zeros((targets, total), jnp.float32)
    for g in range(targets):
        delta = jnp.where((row == g) & (lane == g * positions + pos[g]), 1.0, delta)
    return delta


def share_kernel(
    n_mp,
    n_feat,
    chunk,
    pos,
    dir_ref,
    attn,
    inv_rms,
    gain_ref,
    w_out,
    w_value,
    dec,
    act,
    on,
    z_ref,
    gate_ref,
    c_ref,
    lower,
    dec_v,
    z_v,
    act_v,
    on_v,
    gate_v,
    pair_in,
    acc,
    got,
    dir_full,
    attn_v,
    w_out_v,
    w_full,
    u_all,
    ct_own,
    ct_all,
    pair_sem,
    step_send,
    step_recv,
    full_sem,
    w_sem,
    gather_send,
    gather_recv,
    dec_sem,
    z_sem,
    gate_in_sem,
    gate_out_sem,
):
    mp = lax.axis_index("mp")
    feat = lax.axis_index("feat")
    mine = lax.rem(mp, 2)
    other = 1 - mine
    pair = {"mp": flip(mp, 1)}
    stages = [("feat", b) for b in bits_of(n_feat)] + [("mp", b) for b in bits_of(n_mp)[1:]]
    count, pieces = len(stages), got.shape[1]
    targets = dir_ref.shape[1]
    half = dir_ref.shape[2]
    width = 2 * half
    local_heads = w_out.shape[0]
    kv_heads, columns, head_size = w_value.shape
    heads = local_heads * n_mp

    own_columns = pl.ds(pl.multiple_of(mp * columns, TILE), columns)
    load_attn = pltpu.make_async_copy(attn, attn_v, w_sem.at[2])
    load_out = pltpu.make_async_copy(w_out, w_out_v, w_sem.at[0])
    load_value = pltpu.make_async_copy(w_value, w_full.at[:, own_columns, :], w_sem.at[1])
    load_out.start()
    load_value.start()

    features = dec.shape[1]
    chunks = features // chunk
    lines = gate_v.shape[1]
    parts = act.shape[0] // lines
    points = count + 2

    def load_dec(layer, i):
        at = pl.ds(pl.multiple_of(i * chunk, chunk), chunk)
        return pltpu.make_async_copy(
            dec.at[layer, at, :], dec_v.at[layer, at, :], dec_sem.at[layer, i]
        )

    def load_gate(j):
        at = pl.ds(j * lines, lines)
        return [
            pltpu.make_async_copy(act.at[at, :], act_v.at[j % 2], gate_in_sem.at[0, j]),
            pltpu.make_async_copy(on.at[at, :], on_v.at[j % 2], gate_in_sem.at[1, j]),
        ]

    def store_gate(j):
        return pltpu.make_async_copy(
            gate_v.at[j % 2], gate_ref.at[pl.ds(j * lines, lines), :], gate_out_sem.at[j]
        )

    for copy in load_gate(0):
        copy.start()
    each = -(-2 * chunks // points)

    def beside(j):
        if j + 1 < parts:
            for copy in load_gate(j + 1):
                copy.start()
        for i in range(j * each, min((j + 1) * each, 2 * chunks)):
            load_dec(i % 2, i // 2).start()
        if j < parts:
            for copy in load_gate(j):
                copy.wait()
            if j >= 2:
                store_gate(j - 2).wait()

            def multiply(i, carry):
                at = pl.ds(pl.multiple_of(i * TILE, TILE), TILE)
                gate_v[j % 2, at, :] = (
                    act_v[j % 2, at, :].astype(jnp.float32)
                    * on_v[j % 2, at, :].astype(jnp.float32)
                ).astype(jnp.bfloat16)
                return carry

            lax.fori_loop(0, lines // TILE, multiply, 0)
            store_gate(j).start()

    def partner(stage):
        axis, bit = stages[stage]
        return {axis: flip(feat if axis == "feat" else mp, bit)}

    barrier = pltpu.get_barrier_semaphore()
    greeted = [{"feat": flip(feat, b)} for b in bits_of(n_feat)]
    greeted += [{"mp": lax.rem(mp + o, n_mp)} for o in range(1, n_mp)]
    for device in greeted:
        pl.semaphore_signal(barrier, inc=1, device_id=device, device_id_type=MESH)
    pl.semaphore_wait(barrier, len(greeted))

    def remote(src, dst, send, recv, device):
        copy = pltpu.make_async_remote_copy(
            src_ref=src,
            dst_ref=dst,
            send_sem=send,
            recv_sem=recv,
            device_id=device,
            device_id_type=MESH,
        )
        copy.start()
        return copy

    def gather(kind, src, dst):
        return [
            remote(
                src,
                dst,
                gather_send.at[kind, o - 1],
                gather_recv.at[kind, o - 1],
                {"mp": lax.rem(mp + o, n_mp)},
            )
            for o in range(1, n_mp)
        ]

    first = remote(dir_ref.at[other], pair_in, pair_sem.at[0], pair_sem.at[1], pair)
    values_sent = gather(0, w_value, w_full.at[:, own_columns, :])
    beside(0)
    first.wait()
    start = dir_ref[mine] + pair_in[...]
    size = half // pieces
    for p in range(pieces):
        acc[0, p] = start[:, p * size : (p + 1) * size]
    for k in range(count):
        copies = []
        for p in range(pieces):
            copies.append(
                remote(
                    acc.at[k, p],
                    got.at[k, p],
                    step_send.at[k, p],
                    step_recv.at[k, p],
                    partner((k + p) % count),
                )
            )
        beside(k + 1)
        for p in range(pieces):
            copies[p].wait()
            acc[k + 1, p] = acc[k, p] + got[k, p]
    for p in range(pieces):
        dir_full[mine, :, p * size : (p + 1) * size] = acc[count, p]
    last = remote(
        dir_full.at[mine], dir_full.at[mine], full_sem.at[0], full_sem.at[1], pair
    )
    load_attn.start()
    beside(count + 1)
    load_out.wait()
    last.wait()

    for c in range(2):
        part = dir_full[c]
        lower[pl.ds(heads * targets, targets), pl.ds(c * half, half)] = part
        lower[pl.ds((heads + 1) * targets, targets), pl.ds(c * half, half)] = part
    direction = lower[pl.ds(heads * targets, targets), :]
    own_u = lax.dot_general(
        direction,
        w_out_v[...].reshape(local_heads * head_size, width),
        NT,
        preferred_element_type=jnp.float32,
    ).astype(jnp.bfloat16)
    for l in range(local_heads):
        u_all[mp, l] = own_u[:, l * head_size : (l + 1) * head_size]
    u_sent = gather(2, u_all.at[mp], u_all.at[mp])

    load_attn.wait()
    place_coefficients(pos, attn_v, inv_rms, ct_own)
    coefficients_sent = gather(1, ct_own, ct_all.at[mp])
    ct_all[mp] = ct_own[...]
    load_value.wait()
    for copy in values_sent:
        copy.wait()
    for copy in u_sent:
        copy.wait()
    group = heads // kv_heads
    gain = gain_ref[...].reshape(1, width)
    for kv in range(kv_heads):
        spread = jnp.concatenate(
            [
                u_all[h // local_heads, h % local_heads]
                for h in range(kv * group, (kv + 1) * group)
            ],
            axis=0,
        )
        value = lax.dot_general(spread, w_full[kv], NT, preferred_element_type=jnp.float32)
        lower[pl.ds(kv * group * targets, group * targets), :] = (value * gain).astype(
            jnp.bfloat16
        )


    straight = 2 * targets
    top_row = heads * targets
    lane = lax.broadcasted_iota(jnp.int32, (chunk, straight), 1)

    def store_z(i):
        at = pl.ds(pl.multiple_of(i * chunk, chunk), chunk)
        return pltpu.make_async_copy(z_v.at[at, :], z_ref.at[at, :], z_sem.at[i])

    def score(i, carry):
        at = pl.ds(pl.multiple_of(i * chunk, chunk), chunk)
        load_dec(0, i).wait()
        load_dec(1, i).wait()
        bottom = lax.dot_general(
            dec_v[0, at, :], lower[...], NT, preferred_element_type=jnp.float32
        )
        top = lax.dot_general(
            dec_v[1, at, :],
            lower[pl.ds(top_row, straight), :],
            NT,
            preferred_element_type=jnp.float32,
        )
        z_v[at, pl.ds(0, top_row)] = bottom[:, :top_row].astype(jnp.bfloat16)
        both = bottom[:, top_row:] + top
        high = both.astype(jnp.bfloat16).astype(jnp.float32)
        z_v[at, pl.ds(top_row, straight)] = jnp.where(
            lane < targets, high, both - high
        ).astype(jnp.bfloat16)
        store_z(i).start()
        return carry

    lax.fori_loop(0, chunks, score, 0)
    for copy in coefficients_sent:
        copy.wait()
    delta = target_rows(pos, targets, inv_rms.shape[1])
    coefficients = jnp.concatenate(
        [ct_all[m].astype(jnp.float32) for m in range(n_mp)] + [delta] * 2, axis=0
    )
    c_ref[...] = coefficients.T.astype(jnp.bfloat16)
    for j in range(max(parts - 2, 0), parts):
        store_gate(j).wait()

    def drain(i, carry):
        store_z(i).wait()
        return carry

    lax.fori_loop(0, chunks, drain, 0)


def gate_kernel(c_ref, z_ref, gate_ref, out_ref):
    scores = lax.dot_general(c_ref[...], z_ref[...], NT, preferred_element_type=jnp.float32)
    out_ref[...] = gate_ref[...].astype(jnp.float32) * scores


def on_device(
    n_mp,
    n_feat,
    target_ids,
    target_pos,
    unembed,
    attn_weights,
    inv_rms,
    norm_gain,
    w_value,
    w_out,
    decoder,
    activation,
    active,
):
    vocab_rows, width = unembed.shape
    targets, positions = inv_rms.shape
    local_heads = w_out.shape[0]
    kv_heads, columns, head_size = w_value.shape
    features = decoder.shape[1]
    total = targets * positions
    half = width // 2
    heads = local_heads * n_mp
    rank_rows = heads * targets + 2 * targets
    bf16, f32 = jnp.bfloat16, jnp.float32
    vmem = pl.BlockSpec(memory_space=pltpu.VMEM)
    smem = pl.BlockSpec(memory_space=pltpu.SMEM)
    hbm = pl.BlockSpec(memory_space=pl.ANY)

    if vocab_rows % TILE:
        unembed = jnp.pad(unembed, ((0, TILE - vocab_rows % TILE), (0, 0)))
        rank = lax.axis_index("mp") * n_feat + lax.axis_index("feat")
        local = target_ids - rank * vocab_rows
        inside = (local >= 0) & (local < vocab_rows)
        target_ids = jnp.where(inside, rank * unembed.shape[0] + local, -1)
    direction = pl.pallas_call(
        pick_kernel,
        out_shape=jax.ShapeDtypeStruct((2, targets, half), bf16),
        in_specs=[smem, hbm],
        out_specs=vmem,
        scratch_shapes=[
            pltpu.VMEM((targets * TILE, width), bf16),
            pltpu.SemaphoreType.DMA((targets,)),
        ],
        compiler_params=pltpu.CompilerParams(vmem_limit_bytes=63 * 2**20),
        cost_estimate=pl.CostEstimate(
            flops=2 * targets * targets * TILE * width,
            bytes_accessed=2 * targets * TILE * width,
            transcendentals=0,
        ),
        name="pick_rows",
    )(target_ids, unembed)

    steps = len(bits_of(n_feat)) + len(bits_of(n_mp)) - 1
    pieces = 3 if half % (3 * 128) == 0 else 1
    size = half // pieces
    dma = pltpu.SemaphoreType.DMA
    chunk = chunk_of(features, 512)
    parts = max(
        n for n in range(1, steps + 3) if total % n == 0 and (total // n) % TILE == 0
    )
    lines = total // parts
    z, gate, c = pl.pallas_call(
        functools.partial(share_kernel, n_mp, n_feat, chunk),
        out_shape=(
            jax.ShapeDtypeStruct((features, rank_rows), bf16),
            jax.ShapeDtypeStruct((total, features), bf16),
            jax.ShapeDtypeStruct((total, rank_rows), bf16),
        ),
        in_specs=[smem, vmem, hbm, vmem, vmem, hbm, hbm, hbm, hbm, hbm],
        out_specs=(hbm, hbm, vmem),
        scratch_shapes=[
            pltpu.VMEM((rank_rows, width), bf16),
            pltpu.VMEM(decoder.shape, bf16),
            pltpu.VMEM((features, rank_rows), bf16),
            pltpu.VMEM((2, lines, features), bf16),
            pltpu.VMEM((2, lines, features), jnp.int32),
            pltpu.VMEM((2, lines, features), bf16),
            pltpu.VMEM((targets, half), bf16),
            pltpu.VMEM((steps + 1, pieces, targets, size), bf16),
            pltpu.VMEM((steps, pieces, targets, size), bf16),
            pltpu.VMEM((2, targets, half), bf16),
            pltpu.VMEM(attn_weights.shape, f32),
            pltpu.VMEM(w_out.shape, bf16),
            pltpu.VMEM((kv_heads, columns * n_mp, head_size), bf16),
            pltpu.VMEM((n_mp, local_heads, targets, head_size), bf16),
            pltpu.VMEM((local_heads * targets, total), bf16),
            pltpu.VMEM((n_mp, local_heads * targets, total), bf16),
            dma((2,)),
            dma((steps, pieces)),
            dma((steps, pieces)),
            dma((2,)),
            dma((3,)),
            dma((3, n_mp - 1)),
            dma((3, n_mp - 1)),
            dma((2, features // chunk)),
            dma((features // chunk,)),
            dma((2, parts)),
            dma((parts,)),
        ],
        compiler_params=pltpu.CompilerParams(
            collective_id=0, has_side_effects=True, vmem_limit_bytes=63 * 2**20
        ),
        cost_estimate=pl.CostEstimate(
            flops=2 * features * width * rank_rows,
            bytes_accessed=4 * features * width + 6 * total * features,
            transcendentals=0,
        ),
        name="share",
    )(
        target_pos,
        direction,
        attn_weights,
        inv_rms,
        norm_gain,
        w_out,
        w_value,
        decoder,
        activation.reshape(total, features),
        active.reshape(total, features),
    )

    block = chunk_of(features, 384)
    out = pl.pallas_call(
        gate_kernel,
        grid=(features // block,),
        out_shape=jax.ShapeDtypeStruct((total, features), f32),
        in_specs=[
            pl.BlockSpec((total, rank_rows), lambda i: (0, 0)),
            pl.BlockSpec((block, rank_rows), lambda i: (i, 0)),
            pl.BlockSpec((total, block), lambda i: (0, i)),
        ],
        out_specs=pl.BlockSpec((total, block), lambda i: (0, i)),
        compiler_params=pltpu.CompilerParams(vmem_limit_bytes=63 * 2**20),
        cost_estimate=pl.CostEstimate(
            flops=2 * features * total * rank_rows,
            bytes_accessed=6 * total * features,
            transcendentals=0,
        ),
        name="gate",
    )(c, z, gate)
    return out.reshape(targets, positions, features)


def solution(mesh):
    in_specs = (
        P(),
        P(),
        P(("mp", "feat"), None),
        P("mp", None, None, None),
        P(),
        P(),
        P(None, "mp", None),
        P("mp", None, None),
        P(None, ("mp", "feat"), None),
        P(None, None, ("mp", "feat")),
        P(None, None, ("mp", "feat")),
    )
    out_specs = P(None, None, ("mp", "feat"))
    return jax.shard_map(
        functools.partial(on_device, mesh.shape["mp"], mesh.shape["feat"]),
        mesh=mesh,
        in_specs=in_specs,
        out_specs=out_specs,
        check_vma=False,
    )
```

```python
import functools

import jax
import jax.numpy as jnp
from jax import lax
from jax.experimental import pallas as pl
from jax.experimental.pallas import tpu as pltpu
from jax.sharding import PartitionSpec as P

MESH = pl.DeviceIdType.MESH
NT = (((1,), (1,)), ((), ()))
TILE = 16


def bits_of(n):
    return [1 << b for b in range(n.bit_length() - 1)]


def flip(index, bit):
    return index + bit - 2 * bit * lax.rem(lax.div(index, bit), 2)


def chunk_of(n, most):
    return max(c for c in range(TILE, most + 1, TILE) if n % c == 0)


def pick_kernel(
    ids, pos, unembed, attn, inv_rms, dir_ref, ct_ref, delta_ref, blocks, attn_v, sems, attn_sem
):
    rows, width = unembed.shape
    targets = dir_ref.shape[1]
    half = width // 2
    rank = lax.axis_index("mp") * lax.axis_size("feat") + lax.axis_index("feat")
    first = rank * rows

    def fetch(g):
        local = jnp.clip(ids[g] - first, 0, rows - 1)
        base = pl.multiple_of(lax.div(local, TILE) * TILE, TILE)
        return pltpu.make_async_copy(
            unembed.at[pl.ds(base, TILE), :],
            blocks.at[pl.ds(g * TILE, TILE), :],
            sems.at[g],
        )

    for g in range(targets):
        fetch(g).start()
    load_attn = pltpu.make_async_copy(attn, attn_v, attn_sem)
    load_attn.start()
    delta_ref[...] = target_rows(pos, targets, inv_rms.shape[1]).astype(jnp.bfloat16)
    lane = lax.broadcasted_iota(jnp.int32, (targets, targets * TILE), 1)
    row = lax.broadcasted_iota(jnp.int32, (targets, targets * TILE), 0)
    picker = jnp.zeros((targets, targets * TILE), jnp.float32)
    for g in range(targets):
        local = ids[g] - first
        inside = (local >= 0) & (local < rows)
        at = jnp.where(inside, g * TILE + lax.rem(jnp.maximum(local, 0), TILE), -1)
        picker = jnp.where((row == g) & (lane == at), 1.0, picker)
    for g in range(targets):
        fetch(g).wait()
    picker = picker.astype(jnp.bfloat16)
    for c in range(2):
        dir_ref[c] = jnp.dot(
            picker, blocks[:, pl.ds(c * half, half)], preferred_element_type=jnp.float32
        ).astype(jnp.bfloat16)
    load_attn.wait()
    place_coefficients(pos, attn_v, inv_rms, ct_ref)


def place_coefficients(pos, attn, inv_rms, ct_ref):
    heads, targets, positions, _ = attn.shape
    total = targets * positions
    spots = lax.broadcasted_iota(jnp.int32, (positions, total), 1) - lax.broadcasted_iota(
        jnp.int32, (positions, total), 0
    )
    tile = jnp.zeros((positions, total), jnp.float32)
    for g in range(targets):
        tile = jnp.where(spots == g * positions, 1.0, tile)
    lane = lax.broadcasted_iota(jnp.int32, (targets, total), 1)
    row = lax.broadcasted_iota(jnp.int32, (targets, total), 0)
    own = (lane >= row * positions) & (lane < (row + 1) * positions)
    t_iota = lax.broadcasted_iota(jnp.int32, (positions, positions), 0)
    s_row = lax.broadcasted_iota(jnp.int32, (1, positions), 1)
    for h in range(heads):
        lines = []
        for g in range(targets):
            line = jnp.sum(
                jnp.where(t_iota == pos[g], attn[h, g], 0.0), axis=0, keepdims=True
            )
            lines.append(jnp.where(s_row <= pos[g], line, 0.0))
        weights = jnp.concatenate(lines, axis=0)
        pattern = weights / jnp.sum(weights, axis=-1, keepdims=True) * inv_rms[...]
        spreadout = jnp.dot(
            pattern, tile, precision=lax.Precision.HIGHEST, preferred_element_type=jnp.float32
        )
        ct_ref[pl.ds(h * targets, targets), :] = jnp.where(own, spreadout, 0.0).astype(
            jnp.bfloat16
        )


def target_rows(pos, targets, positions):
    total = targets * positions
    lane = lax.broadcasted_iota(jnp.int32, (targets, total), 1)
    row = lax.broadcasted_iota(jnp.int32, (targets, total), 0)
    delta = jnp.zeros((targets, total), jnp.float32)
    for g in range(targets):
        delta = jnp.where((row == g) & (lane == g * positions + pos[g]), 1.0, delta)
    return delta


def share_kernel(
    n_mp,
    n_feat,
    chunk,
    dir_ref,
    ct_ref,
    delta_ref,
    gain_ref,
    w_out,
    w_value,
    dec,
    act,
    on,
    z_ref,
    gate_ref,
    c_ref,
    lower,
    dec_v,
    z_v,
    act_v,
    on_v,
    gate_v,
    pair_in,
    acc,
    got,
    dir_full,
    w_out_v,
    w_full,
    u_all,
    ct_all,
    d_top,
    pair_sem,
    step_send,
    step_recv,
    full_sem,
    w_sem,
    gather_send,
    gather_recv,
    dec_sem,
    z_sem,
    gate_in_sem,
    gate_out_sem,
):
    mp = lax.axis_index("mp")
    feat = lax.axis_index("feat")
    mine = lax.rem(mp, 2)
    other = 1 - mine
    pair = {"mp": flip(mp, 1)}
    stages = [("feat", b) for b in bits_of(n_feat)] + [("mp", b) for b in bits_of(n_mp)[1:]]
    count, pieces = len(stages), got.shape[1]
    targets = dir_ref.shape[1]
    half = dir_ref.shape[2]
    width = 2 * half
    local_heads = w_out.shape[0]
    kv_heads, columns, head_size = w_value.shape
    heads = local_heads * n_mp

    own_columns = pl.ds(pl.multiple_of(mp * columns, TILE), columns)
    load_out = pltpu.make_async_copy(w_out, w_out_v, w_sem.at[0])
    load_value = pltpu.make_async_copy(w_value, w_full.at[:, own_columns, :], w_sem.at[1])
    load_out.start()
    load_value.start()

    features = dec.shape[1]
    chunks = features // chunk
    lines = gate_v.shape[1]
    parts = act.shape[0] // lines
    points = count + 2

    def load_dec(layer, i):
        at = pl.ds(pl.multiple_of(i * chunk, chunk), chunk)
        return pltpu.make_async_copy(
            dec.at[layer, at, :], dec_v.at[layer, at, :], dec_sem.at[layer, i]
        )

    def load_gate(j):
        at = pl.ds(j * lines, lines)
        return [
            pltpu.make_async_copy(act.at[at, :], act_v.at[j % 2], gate_in_sem.at[0, j]),
            pltpu.make_async_copy(on.at[at, :], on_v.at[j % 2], gate_in_sem.at[1, j]),
        ]

    def store_gate(j):
        return pltpu.make_async_copy(
            gate_v.at[j % 2], gate_ref.at[pl.ds(j * lines, lines), :], gate_out_sem.at[j]
        )

    for copy in load_gate(0):
        copy.start()
    each = -(-2 * chunks // points)

    def beside(j):
        if j + 1 < parts:
            for copy in load_gate(j + 1):
                copy.start()
        for i in range(j * each, min((j + 1) * each, 2 * chunks)):
            load_dec(i % 2, i // 2).start()
        if j < parts:
            for copy in load_gate(j):
                copy.wait()
            if j >= 2:
                store_gate(j - 2).wait()

            def multiply(i, carry):
                at = pl.ds(pl.multiple_of(i * TILE, TILE), TILE)
                gate_v[j % 2, at, :] = (
                    act_v[j % 2, at, :].astype(jnp.float32)
                    * on_v[j % 2, at, :].astype(jnp.float32)
                ).astype(jnp.bfloat16)
                return carry

            lax.fori_loop(0, lines // TILE, multiply, 0)
            store_gate(j).start()

    def partner(stage):
        axis, bit = stages[stage]
        return {axis: flip(feat if axis == "feat" else mp, bit)}

    barrier = pltpu.get_barrier_semaphore()
    greeted = [{"feat": flip(feat, b)} for b in bits_of(n_feat)]
    greeted += [{"mp": lax.rem(mp + o, n_mp)} for o in range(1, n_mp)]
    for device in greeted:
        pl.semaphore_signal(barrier, inc=1, device_id=device, device_id_type=MESH)
    pl.semaphore_wait(barrier, len(greeted))

    def remote(src, dst, send, recv, device):
        copy = pltpu.make_async_remote_copy(
            src_ref=src,
            dst_ref=dst,
            send_sem=send,
            recv_sem=recv,
            device_id=device,
            device_id_type=MESH,
        )
        copy.start()
        return copy

    def gather(kind, src, dst):
        return [
            remote(
                src,
                dst,
                gather_send.at[kind, o - 1],
                gather_recv.at[kind, o - 1],
                {"mp": lax.rem(mp + o, n_mp)},
            )
            for o in range(1, n_mp)
        ]

    first = remote(dir_ref.at[other], pair_in, pair_sem.at[0], pair_sem.at[1], pair)
    coefficients_sent = gather(1, ct_ref, ct_all.at[mp])
    values_sent = gather(0, w_value, w_full.at[:, own_columns, :])
    beside(0)
    first.wait()
    start = dir_ref[mine] + pair_in[...]
    size = half // pieces
    for p in range(pieces):
        acc[0, p] = start[:, p * size : (p + 1) * size]
    for k in range(count):
        copies = []
        for p in range(pieces):
            copies.append(
                remote(
                    acc.at[k, p],
                    got.at[k, p],
                    step_send.at[k, p],
                    step_recv.at[k, p],
                    partner((k + p) % count),
                )
            )
        beside(k + 1)
        for p in range(pieces):
            copies[p].wait()
            acc[k + 1, p] = acc[k, p] + got[k, p]
    for p in range(pieces):
        dir_full[mine, :, p * size : (p + 1) * size] = acc[count, p]
    last = remote(
        dir_full.at[mine], dir_full.at[mine], full_sem.at[0], full_sem.at[1], pair
    )
    beside(count + 1)
    ct_all[mp] = ct_ref[...]
    for copy in coefficients_sent:
        copy.wait()
    coefficients = jnp.concatenate(
        [ct_all[m].astype(jnp.float32) for m in range(n_mp)]
        + [delta_ref[...].astype(jnp.float32)] * 2,
        axis=0,
    )
    c_ref[...] = coefficients.T.astype(jnp.bfloat16)
    load_out.wait()
    last.wait()

    for c in range(2):
        part = dir_full[c]
        lower[pl.ds(heads * targets, targets), pl.ds(c * half, half)] = part
        lower[pl.ds((heads + 1) * targets, targets), pl.ds(c * half, half)] = part
    direction = lower[pl.ds(heads * targets, targets), :]
    own_u = lax.dot_general(
        direction,
        w_out_v[...].reshape(local_heads * head_size, width),
        NT,
        preferred_element_type=jnp.float32,
    ).astype(jnp.bfloat16)
    for l in range(local_heads):
        u_all[mp, l] = own_u[:, l * head_size : (l + 1) * head_size]
    u_sent = gather(2, u_all.at[mp], u_all.at[mp])

    straight = 2 * targets
    top_row = heads * targets

    def top(i, carry):
        at = pl.ds(pl.multiple_of(i * chunk, chunk), chunk)
        load_dec(1, i).wait()
        d_top[at, :] = lax.dot_general(
            dec_v[1, at, :],
            lower[pl.ds(top_row, straight), :],
            NT,
            preferred_element_type=jnp.float32,
        )
        return carry

    early = chunks // 2
    lax.fori_loop(0, early, top, 0)
    load_value.wait()
    for copy in values_sent:
        copy.wait()
    for copy in u_sent:
        copy.wait()
    group = heads // kv_heads
    gain = gain_ref[...].reshape(1, width)
    for kv in range(kv_heads):
        spread = jnp.concatenate(
            [
                u_all[h // local_heads, h % local_heads]
                for h in range(kv * group, (kv + 1) * group)
            ],
            axis=0,
        )
        value = lax.dot_general(spread, w_full[kv], NT, preferred_element_type=jnp.float32)
        lower[pl.ds(kv * group * targets, group * targets), :] = (value * gain).astype(
            jnp.bfloat16
        )


    lax.fori_loop(early, chunks, top, 0)
    lane = lax.broadcasted_iota(jnp.int32, (chunk, straight), 1)

    def store_z(i):
        at = pl.ds(pl.multiple_of(i * chunk, chunk), chunk)
        return pltpu.make_async_copy(z_v.at[at, :], z_ref.at[at, :], z_sem.at[i])

    def score(i, carry):
        at = pl.ds(pl.multiple_of(i * chunk, chunk), chunk)
        load_dec(0, i).wait()
        bottom = lax.dot_general(
            dec_v[0, at, :], lower[...], NT, preferred_element_type=jnp.float32
        )
        z_v[at, pl.ds(0, top_row)] = bottom[:, :top_row].astype(jnp.bfloat16)
        both = bottom[:, top_row:] + d_top[at, :]
        high = both.astype(jnp.bfloat16).astype(jnp.float32)
        z_v[at, pl.ds(top_row, straight)] = jnp.where(
            lane < targets, high, both - high
        ).astype(jnp.bfloat16)
        store_z(i).start()
        return carry

    lax.fori_loop(0, chunks, score, 0)
    for j in range(max(parts - 2, 0), parts):
        store_gate(j).wait()

    def drain(i, carry):
        store_z(i).wait()
        return carry

    lax.fori_loop(0, chunks, drain, 0)


def gate_kernel(c_ref, z_ref, gate_ref, out_ref):
    scores = lax.dot_general(c_ref[...], z_ref[...], NT, preferred_element_type=jnp.float32)
    out_ref[...] = gate_ref[...].astype(jnp.float32) * scores


def on_device(
    n_mp,
    n_feat,
    target_ids,
    target_pos,
    unembed,
    attn_weights,
    inv_rms,
    norm_gain,
    w_value,
    w_out,
    decoder,
    activation,
    active,
):
    vocab_rows, width = unembed.shape
    targets, positions = inv_rms.shape
    local_heads = w_out.shape[0]
    kv_heads, columns, head_size = w_value.shape
    features = decoder.shape[1]
    total = targets * positions
    half = width // 2
    heads = local_heads * n_mp
    rank_rows = heads * targets + 2 * targets
    bf16, f32 = jnp.bfloat16, jnp.float32
    vmem = pl.BlockSpec(memory_space=pltpu.VMEM)
    smem = pl.BlockSpec(memory_space=pltpu.SMEM)
    hbm = pl.BlockSpec(memory_space=pl.ANY)

    if vocab_rows % TILE:
        unembed = jnp.pad(unembed, ((0, TILE - vocab_rows % TILE), (0, 0)))
        rank = lax.axis_index("mp") * n_feat + lax.axis_index("feat")
        local = target_ids - rank * vocab_rows
        inside = (local >= 0) & (local < vocab_rows)
        target_ids = jnp.where(inside, rank * unembed.shape[0] + local, -1)
    direction, coefficients, delta = pl.pallas_call(
        pick_kernel,
        out_shape=(
            jax.ShapeDtypeStruct((2, targets, half), bf16),
            jax.ShapeDtypeStruct((local_heads * targets, total), bf16),
            jax.ShapeDtypeStruct((targets, total), bf16),
        ),
        in_specs=[smem, smem, hbm, hbm, vmem],
        out_specs=(vmem, vmem, vmem),
        scratch_shapes=[
            pltpu.VMEM((targets * TILE, width), bf16),
            pltpu.VMEM(attn_weights.shape, f32),
            pltpu.SemaphoreType.DMA((targets,)),
            pltpu.SemaphoreType.DMA,
        ],
        compiler_params=pltpu.CompilerParams(vmem_limit_bytes=63 * 2**20),
        cost_estimate=pl.CostEstimate(
            flops=2 * targets * targets * TILE * width,
            bytes_accessed=2 * targets * TILE * width,
            transcendentals=0,
        ),
        name="pick_rows",
    )(target_ids, target_pos, unembed, attn_weights, inv_rms)

    steps = len(bits_of(n_feat)) + len(bits_of(n_mp)) - 1
    pieces = 3 if half % (3 * 128) == 0 else 1
    size = half // pieces
    dma = pltpu.SemaphoreType.DMA
    chunk = chunk_of(features, 512)
    parts = max(
        n for n in range(1, steps + 3) if total % n == 0 and (total // n) % TILE == 0
    )
    lines = total // parts
    z, gate, c = pl.pallas_call(
        functools.partial(share_kernel, n_mp, n_feat, chunk),
        out_shape=(
            jax.ShapeDtypeStruct((features, rank_rows), bf16),
            jax.ShapeDtypeStruct((total, features), bf16),
            jax.ShapeDtypeStruct((total, rank_rows), bf16),
        ),
        in_specs=[vmem, vmem, vmem, vmem, hbm, hbm, hbm, hbm, hbm],
        out_specs=(hbm, hbm, vmem),
        scratch_shapes=[
            pltpu.VMEM((rank_rows, width), bf16),
            pltpu.VMEM(decoder.shape, bf16),
            pltpu.VMEM((features, rank_rows), bf16),
            pltpu.VMEM((2, lines, features), bf16),
            pltpu.VMEM((2, lines, features), jnp.int32),
            pltpu.VMEM((2, lines, features), bf16),
            pltpu.VMEM((targets, half), bf16),
            pltpu.VMEM((steps + 1, pieces, targets, size), bf16),
            pltpu.VMEM((steps, pieces, targets, size), bf16),
            pltpu.VMEM((2, targets, half), bf16),
            pltpu.VMEM(w_out.shape, bf16),
            pltpu.VMEM((kv_heads, columns * n_mp, head_size), bf16),
            pltpu.VMEM((n_mp, local_heads, targets, head_size), bf16),
            pltpu.VMEM((n_mp, local_heads * targets, total), bf16),
            pltpu.VMEM((features, 2 * targets), f32),
            dma((2,)),
            dma((steps, pieces)),
            dma((steps, pieces)),
            dma((2,)),
            dma((2,)),
            dma((3, n_mp - 1)),
            dma((3, n_mp - 1)),
            dma((2, features // chunk)),
            dma((features // chunk,)),
            dma((2, parts)),
            dma((parts,)),
        ],
        compiler_params=pltpu.CompilerParams(
            collective_id=0, has_side_effects=True, vmem_limit_bytes=63 * 2**20
        ),
        cost_estimate=pl.CostEstimate(
            flops=2 * features * width * rank_rows,
            bytes_accessed=4 * features * width + 6 * total * features,
            transcendentals=0,
        ),
        name="share",
    )(
        direction,
        coefficients,
        delta,
        norm_gain,
        w_out,
        w_value,
        decoder,
        activation.reshape(total, features),
        active.reshape(total, features),
    )

    block = chunk_of(features, 768)
    out = pl.pallas_call(
        gate_kernel,
        grid=(features // block,),
        out_shape=jax.ShapeDtypeStruct((total, features), f32),
        in_specs=[
            pl.BlockSpec((total, rank_rows), lambda i: (0, 0)),
            pl.BlockSpec((block, rank_rows), lambda i: (i, 0)),
            pl.BlockSpec((total, block), lambda i: (0, i)),
        ],
        out_specs=pl.BlockSpec((total, block), lambda i: (0, i)),
        compiler_params=pltpu.CompilerParams(vmem_limit_bytes=63 * 2**20),
        cost_estimate=pl.CostEstimate(
            flops=2 * features * total * rank_rows,
            bytes_accessed=6 * total * features,
            transcendentals=0,
        ),
        name="gate",
    )(c, z, gate)
    return out.reshape(targets, positions, features)


def solution(mesh):
    in_specs = (
        P(),
        P(),
        P(("mp", "feat"), None),
        P("mp", None, None, None),
        P(),
        P(),
        P(None, "mp", None),
        P("mp", None, None),
        P(None, ("mp", "feat"), None),
        P(None, None, ("mp", "feat")),
        P(None, None, ("mp", "feat")),
    )
    out_specs = P(None, None, ("mp", "feat"))
    return jax.shard_map(
        functools.partial(on_device, mesh.shape["mp"], mesh.shape["feat"]),
        mesh=mesh,
        in_specs=in_specs,
        out_specs=out_specs,
        check_vma=False,
    )
```

```python
import functools

import jax
import jax.numpy as jnp
from jax import lax
from jax.experimental import pallas as pl
from jax.experimental.pallas import tpu as pltpu
from jax.sharding import PartitionSpec as P

MESH = pl.DeviceIdType.MESH
NT = (((1,), (1,)), ((), ()))
TILE = 16


def bits_of(n):
    return [1 << b for b in range(n.bit_length() - 1)]


def flip(index, bit):
    return index + bit - 2 * bit * lax.rem(lax.div(index, bit), 2)


def chunk_of(n, most):
    return max(c for c in range(TILE, most + 1, TILE) if n % c == 0)


def pick_kernel(
    ids, pos, unembed, attn, inv_rms, dir_ref, ct_ref, delta_ref, blocks, attn_v, sems, attn_sem
):
    rows, width = unembed.shape
    targets = dir_ref.shape[1]
    half = width // 2
    rank = lax.axis_index("mp") * lax.axis_size("feat") + lax.axis_index("feat")
    first = rank * rows

    def fetch(g):
        local = jnp.clip(ids[g] - first, 0, rows - 1)
        base = pl.multiple_of(lax.div(local, TILE) * TILE, TILE)
        return pltpu.make_async_copy(
            unembed.at[pl.ds(base, TILE), :],
            blocks.at[pl.ds(g * TILE, TILE), :],
            sems.at[g],
        )

    for g in range(targets):
        fetch(g).start()
    load_attn = pltpu.make_async_copy(attn, attn_v, attn_sem)
    load_attn.start()
    delta_ref[...] = target_rows(pos, targets, inv_rms.shape[1]).astype(jnp.bfloat16)
    lane = lax.broadcasted_iota(jnp.int32, (targets, targets * TILE), 1)
    row = lax.broadcasted_iota(jnp.int32, (targets, targets * TILE), 0)
    picker = jnp.zeros((targets, targets * TILE), jnp.float32)
    for g in range(targets):
        local = ids[g] - first
        inside = (local >= 0) & (local < rows)
        at = jnp.where(inside, g * TILE + lax.rem(jnp.maximum(local, 0), TILE), -1)
        picker = jnp.where((row == g) & (lane == at), 1.0, picker)
    for g in range(targets):
        fetch(g).wait()
    picker = picker.astype(jnp.bfloat16)
    for c in range(2):
        dir_ref[c] = jnp.dot(
            picker, blocks[:, pl.ds(c * half, half)], preferred_element_type=jnp.float32
        ).astype(jnp.bfloat16)
    load_attn.wait()
    place_coefficients(pos, attn_v, inv_rms, ct_ref)


def place_coefficients(pos, attn, inv_rms, ct_ref):
    heads, targets, positions, _ = attn.shape
    total = targets * positions
    spots = lax.broadcasted_iota(jnp.int32, (positions, total), 1) - lax.broadcasted_iota(
        jnp.int32, (positions, total), 0
    )
    tile = jnp.zeros((positions, total), jnp.float32)
    for g in range(targets):
        tile = jnp.where(spots == g * positions, 1.0, tile)
    lane = lax.broadcasted_iota(jnp.int32, (targets, total), 1)
    row = lax.broadcasted_iota(jnp.int32, (targets, total), 0)
    own = (lane >= row * positions) & (lane < (row + 1) * positions)
    t_iota = lax.broadcasted_iota(jnp.int32, (positions, positions), 0)
    s_row = lax.broadcasted_iota(jnp.int32, (1, positions), 1)
    for h in range(heads):
        lines = []
        for g in range(targets):
            line = jnp.sum(
                jnp.where(t_iota == pos[g], attn[h, g], 0.0), axis=0, keepdims=True
            )
            lines.append(jnp.where(s_row <= pos[g], line, 0.0))
        weights = jnp.concatenate(lines, axis=0)
        pattern = weights / jnp.sum(weights, axis=-1, keepdims=True) * inv_rms[...]
        spreadout = jnp.dot(
            pattern, tile, precision=lax.Precision.HIGHEST, preferred_element_type=jnp.float32
        )
        ct_ref[pl.ds(h * targets, targets), :] = jnp.where(own, spreadout, 0.0).astype(
            jnp.bfloat16
        )


def target_rows(pos, targets, positions):
    total = targets * positions
    lane = lax.broadcasted_iota(jnp.int32, (targets, total), 1)
    row = lax.broadcasted_iota(jnp.int32, (targets, total), 0)
    delta = jnp.zeros((targets, total), jnp.float32)
    for g in range(targets):
        delta = jnp.where((row == g) & (lane == g * positions + pos[g]), 1.0, delta)
    return delta


def share_kernel(
    n_mp,
    n_feat,
    chunk,
    dir_ref,
    ct_ref,
    delta_ref,
    gain_ref,
    w_out,
    w_value,
    dec,
    act,
    on,
    z_ref,
    gate_ref,
    c_ref,
    lower,
    dec_v,
    z_v,
    act_v,
    on_v,
    gate_v,
    pair_in,
    acc,
    got,
    dir_full,
    w_out_v,
    w_full,
    u_all,
    ct_all,
    d_top,
    pair_sem,
    step_send,
    step_recv,
    full_sem,
    w_sem,
    gather_send,
    gather_recv,
    dec_sem,
    z_sem,
    gate_in_sem,
    gate_out_sem,
):
    mp = lax.axis_index("mp")
    feat = lax.axis_index("feat")
    mine = lax.rem(mp, 2)
    other = 1 - mine
    pair = {"mp": flip(mp, 1)}
    stages = [("feat", b) for b in bits_of(n_feat)] + [("mp", b) for b in bits_of(n_mp)[1:]]
    count, pieces = len(stages), got.shape[1]
    targets = dir_ref.shape[1]
    half = dir_ref.shape[2]
    width = 2 * half
    local_heads = w_out.shape[0]
    kv_heads, columns, head_size = w_value.shape
    heads = local_heads * n_mp

    own_columns = pl.ds(pl.multiple_of(mp * columns, TILE), columns)
    load_out = pltpu.make_async_copy(w_out, w_out_v, w_sem.at[0])
    load_value = pltpu.make_async_copy(w_value, w_full.at[:, own_columns, :], w_sem.at[1])
    load_out.start()
    load_value.start()

    features = dec.shape[1]
    chunks = features // chunk
    lines = gate_v.shape[1]
    parts = act.shape[0] // lines
    points = count + 2

    def load_dec(layer, i):
        at = pl.ds(pl.multiple_of(i * chunk, chunk), chunk)
        return pltpu.make_async_copy(
            dec.at[layer, at, :], dec_v.at[layer, at, :], dec_sem.at[layer, i]
        )

    def load_gate(j):
        at = pl.ds(j * lines, lines)
        return [
            pltpu.make_async_copy(act.at[at, :], act_v.at[j % 2], gate_in_sem.at[0, j]),
            pltpu.make_async_copy(on.at[at, :], on_v.at[j % 2], gate_in_sem.at[1, j]),
        ]

    def store_gate(j):
        return pltpu.make_async_copy(
            gate_v.at[j % 2], gate_ref.at[pl.ds(j * lines, lines), :], gate_out_sem.at[j]
        )

    for copy in load_gate(0):
        copy.start()
    each = -(-2 * chunks // points)

    def beside(j):
        if j + 1 < parts:
            for copy in load_gate(j + 1):
                copy.start()
        for i in range(j * each, min((j + 1) * each, 2 * chunks)):
            load_dec(i % 2, i // 2).start()
        if j < parts:
            for copy in load_gate(j):
                copy.wait()
            if j >= 2:
                store_gate(j - 2).wait()

            def multiply(i, carry):
                at = pl.ds(pl.multiple_of(i * TILE, TILE), TILE)
                gate_v[j % 2, at, :] = (
                    act_v[j % 2, at, :].astype(jnp.float32)
                    * on_v[j % 2, at, :].astype(jnp.float32)
                ).astype(jnp.bfloat16)
                return carry

            lax.fori_loop(0, lines // TILE, multiply, 0)
            store_gate(j).start()

    def partner(stage):
        axis, bit = stages[stage]
        return {axis: flip(feat if axis == "feat" else mp, bit)}

    barrier = pltpu.get_barrier_semaphore()
    greeted = [{"feat": flip(feat, b)} for b in bits_of(n_feat)]
    greeted += [{"mp": lax.rem(mp + o, n_mp)} for o in range(1, n_mp)]
    for device in greeted:
        pl.semaphore_signal(barrier, inc=1, device_id=device, device_id_type=MESH)
    pl.semaphore_wait(barrier, len(greeted))

    def remote(src, dst, send, recv, device):
        copy = pltpu.make_async_remote_copy(
            src_ref=src,
            dst_ref=dst,
            send_sem=send,
            recv_sem=recv,
            device_id=device,
            device_id_type=MESH,
        )
        copy.start()
        return copy

    def gather(kind, src, dst):
        return [
            remote(
                src,
                dst,
                gather_send.at[kind, o - 1],
                gather_recv.at[kind, o - 1],
                {"mp": lax.rem(mp + o, n_mp)},
            )
            for o in range(1, n_mp)
        ]

    first = remote(dir_ref.at[other], pair_in, pair_sem.at[0], pair_sem.at[1], pair)
    coefficients_sent = gather(1, ct_ref, ct_all.at[mp])
    values_sent = gather(0, w_value, w_full.at[:, own_columns, :])
    beside(0)
    first.wait()
    start = dir_ref[mine] + pair_in[...]
    size = half // pieces
    for p in range(pieces):
        acc[0, p] = start[:, p * size : (p + 1) * size]
    for k in range(count):
        copies = []
        for p in range(pieces):
            copies.append(
                remote(
                    acc.at[k, p],
                    got.at[k, p],
                    step_send.at[k, p],
                    step_recv.at[k, p],
                    partner((k + p) % count),
                )
            )
        beside(k + 1)
        for p in range(pieces):
            copies[p].wait()
            acc[k + 1, p] = acc[k, p] + got[k, p]
    for p in range(pieces):
        dir_full[mine, :, p * size : (p + 1) * size] = acc[count, p]
    last = remote(
        dir_full.at[mine], dir_full.at[mine], full_sem.at[0], full_sem.at[1], pair
    )
    beside(count + 1)
    ct_all[mp] = ct_ref[...]
    for copy in coefficients_sent:
        copy.wait()
    coefficients = jnp.concatenate(
        [ct_all[m].astype(jnp.float32) for m in range(n_mp)]
        + [delta_ref[...].astype(jnp.float32)] * 2,
        axis=0,
    )
    c_ref[...] = coefficients.T.astype(jnp.bfloat16)
    load_out.wait()
    last.wait()

    for c in range(2):
        part = dir_full[c]
        lower[pl.ds(heads * targets, targets), pl.ds(c * half, half)] = part
        lower[pl.ds((heads + 1) * targets, targets), pl.ds(c * half, half)] = part
    direction = lower[pl.ds(heads * targets, targets), :]
    own_u = lax.dot_general(
        direction,
        w_out_v[...].reshape(local_heads * head_size, width),
        NT,
        preferred_element_type=jnp.float32,
    ).astype(jnp.bfloat16)
    for l in range(local_heads):
        u_all[mp, l] = own_u[:, l * head_size : (l + 1) * head_size]
    u_sent = gather(2, u_all.at[mp], u_all.at[mp])

    straight = 2 * targets
    top_row = heads * targets

    def top(i, carry):
        at = pl.ds(pl.multiple_of(i * chunk, chunk), chunk)
        load_dec(1, i).wait()
        d_top[at, :] = lax.dot_general(
            dec_v[1, at, :],
            lower[pl.ds(top_row, straight), :],
            NT,
            preferred_element_type=jnp.float32,
        )
        return carry

    lax.fori_loop(0, chunks, top, 0)
    load_value.wait()
    for copy in values_sent:
        copy.wait()
    for copy in u_sent:
        copy.wait()
    group = heads // kv_heads
    gain = gain_ref[...].reshape(1, width)
    for kv in range(kv_heads):
        spread = jnp.concatenate(
            [
                u_all[h // local_heads, h % local_heads]
                for h in range(kv * group, (kv + 1) * group)
            ],
            axis=0,
        )
        value = lax.dot_general(spread, w_full[kv], NT, preferred_element_type=jnp.float32)
        lower[pl.ds(kv * group * targets, group * targets), :] = (value * gain).astype(
            jnp.bfloat16
        )


    lane = lax.broadcasted_iota(jnp.int32, (chunk, straight), 1)

    def store_z(i):
        at = pl.ds(pl.multiple_of(i * chunk, chunk), chunk)
        return pltpu.make_async_copy(z_v.at[at, :], z_ref.at[at, :], z_sem.at[i])

    def score(i, carry):
        at = pl.ds(pl.multiple_of(i * chunk, chunk), chunk)
        load_dec(0, i).wait()
        bottom = lax.dot_general(
            dec_v[0, at, :], lower[...], NT, preferred_element_type=jnp.float32
        )
        z_v[at, pl.ds(0, top_row)] = bottom[:, :top_row].astype(jnp.bfloat16)
        both = bottom[:, top_row:] + d_top[at, :]
        high = both.astype(jnp.bfloat16).astype(jnp.float32)
        z_v[at, pl.ds(top_row, straight)] = jnp.where(
            lane < targets, high, both - high
        ).astype(jnp.bfloat16)
        store_z(i).start()
        return carry

    lax.fori_loop(0, chunks, score, 0)
    for j in range(max(parts - 2, 0), parts):
        store_gate(j).wait()

    def drain(i, carry):
        store_z(i).wait()
        return carry

    lax.fori_loop(0, chunks, drain, 0)


def gate_kernel(c_ref, z_ref, gate_ref, out_ref):
    scores = lax.dot_general(c_ref[...], z_ref[...], NT, preferred_element_type=jnp.float32)
    out_ref[...] = gate_ref[...].astype(jnp.float32) * scores


def on_device(
    n_mp,
    n_feat,
    target_ids,
    target_pos,
    unembed,
    attn_weights,
    inv_rms,
    norm_gain,
    w_value,
    w_out,
    decoder,
    activation,
    active,
):
    vocab_rows, width = unembed.shape
    targets, positions = inv_rms.shape
    local_heads = w_out.shape[0]
    kv_heads, columns, head_size = w_value.shape
    features = decoder.shape[1]
    total = targets * positions
    half = width // 2
    heads = local_heads * n_mp
    rank_rows = heads * targets + 2 * targets
    bf16, f32 = jnp.bfloat16, jnp.float32
    vmem = pl.BlockSpec(memory_space=pltpu.VMEM)
    smem = pl.BlockSpec(memory_space=pltpu.SMEM)
    hbm = pl.BlockSpec(memory_space=pl.ANY)

    if vocab_rows % TILE:
        unembed = jnp.pad(unembed, ((0, TILE - vocab_rows % TILE), (0, 0)))
        rank = lax.axis_index("mp") * n_feat + lax.axis_index("feat")
        local = target_ids - rank * vocab_rows
        inside = (local >= 0) & (local < vocab_rows)
        target_ids = jnp.where(inside, rank * unembed.shape[0] + local, -1)
    direction, coefficients, delta = pl.pallas_call(
        pick_kernel,
        out_shape=(
            jax.ShapeDtypeStruct((2, targets, half), bf16),
            jax.ShapeDtypeStruct((local_heads * targets, total), bf16),
            jax.ShapeDtypeStruct((targets, total), bf16),
        ),
        in_specs=[smem, smem, hbm, hbm, vmem],
        out_specs=(vmem, vmem, vmem),
        scratch_shapes=[
            pltpu.VMEM((targets * TILE, width), bf16),
            pltpu.VMEM(attn_weights.shape, f32),
            pltpu.SemaphoreType.DMA((targets,)),
            pltpu.SemaphoreType.DMA,
        ],
        compiler_params=pltpu.CompilerParams(vmem_limit_bytes=63 * 2**20),
        cost_estimate=pl.CostEstimate(
            flops=2 * targets * targets * TILE * width,
            bytes_accessed=2 * targets * TILE * width,
            transcendentals=0,
        ),
        name="pick_rows",
    )(target_ids, target_pos, unembed, attn_weights, inv_rms)

    steps = len(bits_of(n_feat)) + len(bits_of(n_mp)) - 1
    pieces = 3 if half % (3 * 128) == 0 else 1
    size = half // pieces
    dma = pltpu.SemaphoreType.DMA
    chunk = chunk_of(features, 1024)
    parts = max(
        n for n in range(1, steps + 3) if total % n == 0 and (total // n) % TILE == 0
    )
    lines = total // parts
    z, gate, c = pl.pallas_call(
        functools.partial(share_kernel, n_mp, n_feat, chunk),
        out_shape=(
            jax.ShapeDtypeStruct((features, rank_rows), bf16),
            jax.ShapeDtypeStruct((total, features), bf16),
            jax.ShapeDtypeStruct((total, rank_rows), bf16),
        ),
        in_specs=[vmem, vmem, vmem, vmem, hbm, hbm, hbm, hbm, hbm],
        out_specs=(hbm, hbm, vmem),
        scratch_shapes=[
            pltpu.VMEM((rank_rows, width), bf16),
            pltpu.VMEM(decoder.shape, bf16),
            pltpu.VMEM((features, rank_rows), bf16),
            pltpu.VMEM((2, lines, features), bf16),
            pltpu.VMEM((2, lines, features), jnp.int32),
            pltpu.VMEM((2, lines, features), bf16),
            pltpu.VMEM((targets, half), bf16),
            pltpu.VMEM((steps + 1, pieces, targets, size), bf16),
            pltpu.VMEM((steps, pieces, targets, size), bf16),
            pltpu.VMEM((2, targets, half), bf16),
            pltpu.VMEM(w_out.shape, bf16),
            pltpu.VMEM((kv_heads, columns * n_mp, head_size), bf16),
            pltpu.VMEM((n_mp, local_heads, targets, head_size), bf16),
            pltpu.VMEM((n_mp, local_heads * targets, total), bf16),
            pltpu.VMEM((features, 2 * targets), f32),
            dma((2,)),
            dma((steps, pieces)),
            dma((steps, pieces)),
            dma((2,)),
            dma((2,)),
            dma((3, n_mp - 1)),
            dma((3, n_mp - 1)),
            dma((2, features // chunk)),
            dma((features // chunk,)),
            dma((2, parts)),
            dma((parts,)),
        ],
        compiler_params=pltpu.CompilerParams(
            collective_id=0, has_side_effects=True, vmem_limit_bytes=63 * 2**20
        ),
        cost_estimate=pl.CostEstimate(
            flops=2 * features * width * rank_rows,
            bytes_accessed=4 * features * width + 6 * total * features,
            transcendentals=0,
        ),
        name="share",
    )(
        direction,
        coefficients,
        delta,
        norm_gain,
        w_out,
        w_value,
        decoder,
        activation.reshape(total, features),
        active.reshape(total, features),
    )

    block = chunk_of(features, 768)
    out = pl.pallas_call(
        gate_kernel,
        grid=(features // block,),
        out_shape=jax.ShapeDtypeStruct((total, features), f32),
        in_specs=[
            pl.BlockSpec((total, rank_rows), lambda i: (0, 0)),
            pl.BlockSpec((block, rank_rows), lambda i: (i, 0)),
            pl.BlockSpec((total, block), lambda i: (0, i)),
        ],
        out_specs=pl.BlockSpec((total, block), lambda i: (0, i)),
        compiler_params=pltpu.CompilerParams(vmem_limit_bytes=63 * 2**20),
        cost_estimate=pl.CostEstimate(
            flops=2 * features * total * rank_rows,
            bytes_accessed=6 * total * features,
            transcendentals=0,
        ),
        name="gate",
    )(c, z, gate)
    return out.reshape(targets, positions, features)


def solution(mesh):
    in_specs = (
        P(),
        P(),
        P(("mp", "feat"), None),
        P("mp", None, None, None),
        P(),
        P(),
        P(None, "mp", None),
        P("mp", None, None),
        P(None, ("mp", "feat"), None),
        P(None, None, ("mp", "feat")),
        P(None, None, ("mp", "feat")),
    )
    out_specs = P(None, None, ("mp", "feat"))
    return jax.shard_map(
        functools.partial(on_device, mesh.shape["mp"], mesh.shape["feat"]),
        mesh=mesh,
        in_specs=in_specs,
        out_specs=out_specs,
        check_vma=False,
    )
```
